128 devices in a mesh: blk: 8 (over z, y_hi), tok: 16 (over x, y_lo, core).
Axes of the slice: x: 4, y: 4 (y_hi: 2, y_lo: 2; y = y_hi * 2 + y_lo), z: 4, core: 2. Of those that a mesh axis runs over, the one named last changes fastest.
Arguments:
- inputs: float32 [4096, 16384], P('tok', 'blk'), may hold values from -6 to 6
- first_factor: float32 [16, 1024, 1024], P('blk', 'tok'), may hold values from -0.1875 to 0.1875
- second_factor: float32 [16, 1024, 1024], P('blk', 'tok'), may hold values from -0.1875 to 0.1875
- cotangent: float32 [4096, 16384], P('tok', 'blk'), may hold values from -6 to 6
Outputs:
- input_grad: float32 [4096, 16384], P('tok', 'blk')
- first_grad: float32 [16, 1024, 1024], P('blk', 'tok')
- second_grad: float32 [16, 1024, 1024], P('blk', 'tok')
The draws below stay inside these ranges and needn't reach their ends.
All inputs are finite; a program needn't handle non-finite values.
Results may differ from the reference program's by a relative error of at most 0.00013.
Values sent between devices are 32-bit elements; how exact they have to be, the bound alone decides.
A program may use at most 128 MiB of HBM per device.

```python
import jax
import jax.numpy as jnp
from jax import lax

BLOCKS = 16
BS = 1024
FEATURES = 16384
TOKENS = 4096


def level_of(rng, dims, pieces, least, largest):
    def one(dim, parts):
        draws = jax.random.uniform(jax.random.fold_in(jax.random.fold_in(rng, 6), dim), (parts,), jnp.float32, least / len(pieces), largest / len(pieces))
        return jnp.repeat(jnp.exp(draws), dims[dim] // parts).reshape((-1,) + (1,) * (len(dims) - dim - 1))

    level = one(*pieces[0])
    for cut in pieces[1:]:
        level = level * one(*cut)
    return level


def centred(stream_key, shape, width, most, pieces=(), dtype=jnp.bfloat16):
    entries = jax.random.normal(stream_key, shape, jnp.float32) * width
    if len(pieces) > 0:
        entries = level_of(stream_key, shape, pieces, -0.22, 0.18) * entries
    return jnp.clip(entries, min=-most, max=most).astype(dtype)


def setup_inputs(seed: int = 0) -> dict:
    key_of = jax.random.split(jax.random.key(seed), 5)
    return {
        "inputs": centred(key_of[0], (TOKENS, FEATURES), 1.0, 6.0, ((0, 16), (1, 8)), jnp.float32),
        "first_factor": centred(key_of[1], (BLOCKS, BS, BS), BS ** -0.5, 0.1875, ((0, 8), (1, 16)), jnp.float32),
        "second_factor": centred(key_of[2], (BLOCKS, BS, BS), BS ** -0.5, 0.1875, ((0, 8), (1, 16)), jnp.float32),
        "cotangent": centred(key_of[3], (TOKENS, FEATURES), 1.0, 6.0, ((0, 16), (1, 8)), jnp.float32),
    }


def forward(inputs, first_factor, second_factor):
    hp = lax.Precision.HIGHEST
    count = inputs.shape[0]
    group = BS // BLOCKS
    xb = inputs.reshape(count, BLOCKS, BS)
    first = jnp.einsum('tbi,bio->tbo', xb, first_factor, precision=hp)
    mixed = first.reshape(count, BLOCKS, BLOCKS, group).transpose(0, 2, 1, 3).reshape(count, BLOCKS, BS)
    second = jnp.einsum('tsk,sko->tso', mixed, second_factor, precision=hp)
    return jax.nn.gelu(second, approximate=False).reshape(count, BLOCKS * BS)

def reference(inputs, first_factor, second_factor, cotangent):
    outputs, pullback = jax.vjp(forward, inputs, first_factor, second_factor)
    input_grad, first_grad, second_grad = pullback(cotangent)
    return (input_grad, first_grad, second_grad)
```

```python
import math

import jax
import jax.numpy as jnp
from jax import lax
from jax.experimental import pallas as pl
from jax.experimental.pallas import tpu as pltpu
from jax.sharding import PartitionSpec as P

F32 = jnp.float32
BF16 = jnp.bfloat16
XS = 4
NN = (((1,), (0,)), ((), ()))
NT = (((1,), (1,)), ((), ()))
AG_OVER_Y = (True, False)
RS_OVER_Y = (True, False)


def halves(v):
    high = v.astype(BF16)
    return high, (v - high.astype(F32)).astype(BF16)


def product(ah, al, bh, bl, dims):
    def dot(a, b):
        return lax.dot_general(a, b, dims, preferred_element_type=F32)

    return dot(ah, bh) + (dot(ah, bl) + dot(al, bh))


def rows_at(index, size):
    return pl.ds(pl.multiple_of(index * size, size), size)


def kernel(
    x_hbm, w1_hbm, w2_hbm, cot_hbm, dx_hbm, g1_hbm, g2_hbm,
    wbuf, wh, wl, xs, cs, ah, al, xth, xtl, ft, mt, mth, mtl, d2h, d2l, dmt, d1t, rbuf,
    loc_sem, pair_send, pair_recv, ag_send, ag_recv, a2a_send, a2a_recv, rs_send, rs_recv,
):
    w_hbm = (w1_hbm, w2_hbm)
    g_hbm = (g1_hbm, g2_hbm)
    k = lax.axis_index("blk")
    t = lax.axis_index("tok")
    x = t // 4
    y = (t // 2) % 2
    c = t % 2
    oc = 1 - c
    count = x_hbm.shape[0]
    slab = w1_hbm.shape[1]
    order = w1_hbm.shape[2]
    chip = 2 * count
    group = order // 16

    def tok(dx, other_y, core):
        yy = 1 - y if other_y else y
        return {"tok": ((x + dx) % XS) * 4 + yy * 2 + core}

    def slab_of(dx, other_y, core):
        return tok(dx, other_y, core)["tok"]

    def remote(src, dst, send, recv, to):
        return pltpu.make_async_remote_copy(
            src_ref=src, dst_ref=dst, send_sem=send, recv_sem=recv, device_id=to, device_id_type=pl.DeviceIdType.MESH
        )

    mine = rows_at(c, order)
    theirs = rows_at(oc, order)
    own = rows_at(c, count)
    local = [
        pltpu.make_async_copy(x_hbm.at[:, mine], xs.at[own], loc_sem.at[0]),
        pltpu.make_async_copy(cot_hbm.at[:, mine], cs.at[own], loc_sem.at[1]),
        pltpu.make_async_copy(w1_hbm.at[c], wbuf.at[0, rows_at(t, slab)], loc_sem.at[2]),
        pltpu.make_async_copy(w2_hbm.at[c], wbuf.at[1, rows_at(t, slab)], loc_sem.at[3]),
    ]
    for cp in local:
        cp.start()

    barrier = pltpu.get_barrier_semaphore()
    near = [tok(1, False, c), tok(-1 + XS, False, c), tok(0, True, c), tok(0, False, oc)]
    near += [tok(1, False, oc), tok(-1 + XS, False, oc), tok(0, True, oc)]
    for to in near:
        pl.semaphore_signal(barrier, inc=1, device_id=to, device_id_type=pl.DeviceIdType.MESH)

    def greet(i, _):
        kk = (k + 1 + i // 2) % 8
        pl.semaphore_signal(
            barrier, inc=1, device_id={"blk": kk, "tok": t - c + i % 2}, device_id_type=pl.DeviceIdType.MESH
        )
        return 0

    lax.fori_loop(0, 14, greet, 0)
    pl.semaphore_wait(barrier, 14 + len(near))

    def ag(f, n, src, row, to):
        return remote(src, wbuf.at[f, rows_at(row, slab)], ag_send.at[f, n], ag_recv.at[f, row], to)

    def forward(f, n, row, to):
        cp = ag(f, n, wbuf.at[f, rows_at(row, slab)], row, to)
        cp.start()

    def ag_first(f):
        for h in range(2):
            ag(f, h, w_hbm[f].at[h], t, tok(1, False, h)).start()
            ag(f, 2 + h, w_hbm[f].at[h], t, tok(XS - 1, False, h)).start()
            ag(f, 4 + h, w_hbm[f].at[h], t, tok(0, True, h)).start()
        ag(f, 6, w_hbm[f].at[oc], t, tok(0, False, oc)).start()

    def ag_wait(f, row):
        ag(f, 0, wbuf.at[f, rows_at(row, slab)], row, tok(1, False, c)).wait_recv()

    def ag_second(f):
        low, high = slab_of(XS - 1, False, 0), slab_of(1, False, 1)
        ag_wait(f, low)
        forward(f, 7, low, tok(1, False, c))
        ag_wait(f, high)
        forward(f, 8, high, tok(XS - 1, False, c))
        for h in range(2):
            row = slab_of(0, True, h)
            ag_wait(f, row)
            forward(f, 9 + h, row, tok(1, False, c))
            forward(f, 11 + h, row, tok(XS - 1, False, c))

    def ag_third(f):
        if AG_OVER_Y[f]:
            for h in range(2):
                row = slab_of(2, False, h)
                ag_wait(f, row)
                forward(f, 13 + h, row, tok(0, True, c))
        else:
            low, high = slab_of(XS - 1, True, 0), slab_of(1, True, 1)
            ag_wait(f, low)
            forward(f, 13, low, tok(1, False, c))
            ag_wait(f, high)
            forward(f, 14, high, tok(XS - 1, False, c))

    def ag_rest(f):
        ag_wait(f, slab_of(0, False, oc))
        ag_wait(f, slab_of(XS - 1, False, 1))
        ag_wait(f, slab_of(1, False, 0))
        if AG_OVER_Y[f]:
            for h in range(2):
                ag_wait(f, slab_of(1, True, h))
                ag_wait(f, slab_of(XS - 1, True, h))
        else:
            for h in range(2):
                ag_wait(f, slab_of(2, False, h))
            ag_wait(f, slab_of(XS - 1, True, 1))
            ag_wait(f, slab_of(1, True, 0))
        for h in range(2):
            ag_wait(f, slab_of(2, True, h))

    def ag_sent(f):
        for n in range(15):
            ag(f, n, wbuf.at[f, rows_at(t, slab)], t, tok(1, False, c)).wait_send()

    def split_factor(f):
        def step(i, _):
            at = rows_at(i, 128)
            high, low = halves(wbuf[f, at, :])
            wh[f, at, :] = high
            wl[f, at, :] = low
            return 0

        lax.fori_loop(0, order // 128, step, 0)

    ag_first(0)
    pair = tok(0, False, oc)
    swap = [
        remote(x_hbm.at[:, theirs], xs.at[own], pair_send.at[0], pair_recv.at[0], pair),
        remote(cot_hbm.at[:, theirs], cs.at[own], pair_send.at[1], pair_recv.at[1], pair),
    ]
    for cp in swap:
        cp.start()
    for cp in local:
        cp.wait()
    for cp in swap:
        cp.wait()

    def split_x(i, _):
        at = rows_at(i, 128)
        high, low = halves(xs[:, at])
        ah[:, at] = high
        al[:, at] = low
        high, low = halves(xs[:, at].T)
        xth[at, :] = high
        xtl[at, :] = low
        return 0

    lax.fori_loop(0, order // 128, split_x, 0)

    ag_second(0)
    ag_third(0)
    ag_first(1)
    ag_rest(0)
    split_factor(0)

    me = 2 * k + c
    base = t - c

    def a2a(n, src, dst, s):
        return remote(
            src.at[rows_at(s, group)], dst.at[rows_at(me, group)], a2a_send.at[n, s], a2a_recv.at[n, me],
            {"blk": s // 2, "tok": base + s % 2},
        )

    def a2a_start(n, src, dst, s):
        @pl.when(s != me)
        def _():
            a2a(n, src, dst, s).start()

        @pl.when(s == me)
        def _():
            dst[rows_at(me, group), :] = src[rows_at(me, group), :]

    def a2a_wait(n, src, dst):
        def step(s, _):
            @pl.when(s != me)
            def _():
                remote(
                    src.at[rows_at(s, group)], dst.at[rows_at(s, group)], a2a_send.at[n, s], a2a_recv.at[n, s],
                    {"blk": s // 2, "tok": base + s % 2},
                ).wait_recv()

            return 0

        lax.fori_loop(0, 16, step, 0)

    def a2a_sent(n, src, dst):
        def step(s, _):
            @pl.when(s != me)
            def _():
                a2a(n, src, dst, s).wait_send()

            return 0

        lax.fori_loop(0, 16, step, 0)

    z = k // 2

    def first_step(i, _):
        q = (z + 1 + i) % 4
        at = rows_at(q, 256)
        part = product(ah[...], al[...], wh[0, :, at], wl[0, :, at], NN)
        ft[at, :] = part.T
        for r in range(4):
            a2a_start(0, ft, mt, 4 * q + r)
        return 0

    lax.fori_loop(0, 4, first_step, 0)

    ag_second(1)
    ag_third(1)
    ag_rest(1)
    split_factor(1)
    a2a_wait(0, ft, mt)

    def turn(src, keep):
        def step(i, _):
            at = rows_at(i, 128)
            v = src[at, :]
            if keep:
                high, low = halves(v)
                mth[at, :] = high
                mtl[at, :] = low
            high, low = halves(v.T)
            ah[:, at] = high
            al[:, at] = low
            return 0

        lax.fori_loop(0, order // 128, step, 0)

    turn(mt, True)

    def second_step(i, _):
        at = rows_at(i, 256)
        v = product(ah[...], al[...], wh[1, :, at], wl[1, :, at], NN)
        cdf = 0.5 * (1.0 + lax.erf(v * (1.0 / math.sqrt(2.0))))
        density = jnp.exp(-0.5 * v * v) * (1.0 / math.sqrt(2.0 * math.pi))
        high, low = halves(cs[:, at] * (cdf + v * density))
        d2h[:, at] = high
        d2l[:, at] = low
        return 0

    lax.fori_loop(0, 4, second_step, 0)

    def mixed_step(i, _):
        q = (z + 1 + i) % 4
        at = rows_at(q, 256)
        dmt[at, :] = product(wh[1, at, :], wl[1, at, :], d2h[...], d2l[...], NT)
        for r in range(4):
            a2a_start(1, dmt, d1t, 4 * q + r)
        return 0

    lax.fori_loop(0, 4, mixed_step, 0)

    def rs(f, slot, row, to):
        return remote(
            wbuf.at[f, rows_at(row, slab)], rbuf.at[f, slot], rs_send.at[f, slot], rs_recv.at[f, slot], to
        )

    def rs_start(f, slot, row):
        if slot in (1, 2, 3, 7, 8, 9) and not (RS_OVER_Y[f] and slot == 1):
            to = tok(1, False, c)
        elif slot in (0, 1, 12, 13) and (RS_OVER_Y[f] or slot >= 12):
            to = tok(0, True, c)
        else:
            to = tok(XS - 1, False, c)
        rs(f, slot, row, to).start()

    def rs_add(f, row, slots):
        for slot in slots:
            rs(f, slot, t, tok(1, False, c)).wait_recv()
        at = rows_at(row, slab)
        total = rbuf[f, slots[0]]
        for slot in slots[1:]:
            total = total + rbuf[f, slot]
        wbuf[f, at, :] = wbuf[f, at, :] + total

    def gradient(f, lh, ll, rh, rl):
        for dx in (2, 1, 3, 0):
            at = rows_at((x + dx) % XS, 256)
            wbuf[f, at, :] = product(lh[at, :], ll[at, :], rh[...], rl[...], NN)
            if dx == 2:
                if RS_OVER_Y[f]:
                    rs_start(f, 0, slab_of(2, True, 0))
                    rs_start(f, 1, slab_of(2, True, 1))
                else:
                    rs_start(f, 6, slab_of(2, False, 0))
                    rs_start(f, 7, slab_of(2, False, 1))
                    rs_start(f, 0, slab_of(2, True, 0))
                    rs_start(f, 1, slab_of(2, True, 1))
            elif dx == 1:
                rs_start(f, 2, slab_of(1, True, 0))
                if RS_OVER_Y[f]:
                    rs_start(f, 3, slab_of(1, True, 1))
                rs_start(f, 8, slab_of(1, False, 0))
            elif dx == 3:
                rs_start(f, 5, slab_of(3, True, 1))
                if RS_OVER_Y[f]:
                    rs_start(f, 4, slab_of(3, True, 0))
                rs_start(f, 11, slab_of(3, False, 1))

    def rs_middle(f):
        if RS_OVER_Y[f]:
            for h in range(2):
                row = slab_of(2, False, h)
                rs_add(f, row, (h,))
                rs_start(f, 6 + h, row)
        else:
            row = slab_of(1, True, 1)
            rs_add(f, row, (1,))
            rs_start(f, 3, row)
            row = slab_of(3, True, 0)
            rs_add(f, row, (0,))
            rs_start(f, 4, row)
        row = slab_of(1, False, 1)
        rs_add(f, row, (7,))
        rs_start(f, 9, row)
        row = slab_of(3, False, 0)
        rs_add(f, row, (6,))
        rs_start(f, 10, row)
        for h in range(2):
            row = slab_of(0, True, h)
            rs_add(f, row, (2 + h, 4 + h))
            rs_start(f, 12 + h, row)

    def out_local(f):
        return pltpu.make_async_copy(wbuf.at[f, rows_at(t, slab)], g_hbm[f].at[c], loc_sem.at[f])

    def out_pair(f):
        return remote(
            wbuf.at[f, rows_at(base + oc, slab)], g_hbm[f].at[c], rs_send.at[f, 14], rs_recv.at[f, 14], pair
        )

    def out_wait(f):
        return remote(
            wbuf.at[f, rows_at(base + oc, slab)], g_hbm[f].at[oc], rs_send.at[f, 14], rs_recv.at[f, 14], pair
        )

    def rs_end(f):
        for h in range(2):
            rs_add(f, slab_of(0, False, h), (8 + h, 10 + h, 12 + h))
        out_pair(f).start()
        out_local(f).start()

    def rs_done(f):
        out_local(f).wait()
        out_pair(f).wait_send()
        out_wait(f).wait_recv()
        for slot in range(14):
            rs(f, slot, t, tok(1, False, c)).wait_send()

    ag_sent(1)
    gradient(1, mth, mtl, d2h, d2l)
    rs_middle(1)
    a2a_wait(1, dmt, d1t)
    turn(d1t, False)
    ag_sent(0)
    gradient(0, xth, xtl, ah, al)

    def input_step(i, _):
        at = rows_at(i, 256)
        xs[:, at] = product(ah[...], al[...], wh[0, at, :], wl[0, at, :], NT)
        return 0

    lax.fori_loop(0, 4, input_step, 0)
    dx_pair = remote(xs.at[rows_at(oc, count)], dx_hbm.at[:, mine], pair_send.at[2], pair_recv.at[2], pair)
    dx_wait = remote(xs.at[rows_at(oc, count)], dx_hbm.at[:, theirs], pair_send.at[2], pair_recv.at[2], pair)
    dx_local = pltpu.make_async_copy(xs.at[own], dx_hbm.at[:, mine], loc_sem.at[2])
    dx_pair.start()
    dx_local.start()
    rs_end(1)
    rs_middle(0)
    rs_end(0)
    dx_local.wait()
    dx_pair.wait_send()
    dx_wait.wait_recv()
    a2a_sent(0, ft, mt)
    a2a_sent(1, dmt, d1t)
    rs_done(1)
    rs_done(0)


def body(inputs, first_factor, second_factor, cotangent):
    count, width = inputs.shape
    blocks, slab, order = first_factor.shape
    chip = 2 * count
    wide = (chip, order)
    tall = (order, chip)
    dma = pltpu.SemaphoreType.DMA
    return pl.pallas_call(
        kernel,
        out_shape=(
            jax.ShapeDtypeStruct((count, width), F32),
            jax.ShapeDtypeStruct((blocks, slab, order), F32),
            jax.ShapeDtypeStruct((blocks, slab, order), F32),
        ),
        in_specs=[pl.BlockSpec(memory_space=pl.ANY)] * 4,
        out_specs=[pl.BlockSpec(memory_space=pl.ANY)] * 3,
        scratch_shapes=[
            pltpu.VMEM((2, order, order), F32),
            pltpu.VMEM((2, order, order), BF16),
            pltpu.VMEM((2, order, order), BF16),
            pltpu.VMEM(wide, F32),
            pltpu.VMEM(wide, F32),
            pltpu.VMEM(wide, BF16),
            pltpu.VMEM(wide, BF16),
            pltpu.VMEM(tall, BF16),
            pltpu.VMEM(tall, BF16),
            pltpu.VMEM(tall, F32),
            pltpu.VMEM(tall, F32),
            pltpu.VMEM(tall, BF16),
            pltpu.VMEM(tall, BF16),
            pltpu.VMEM(wide, BF16),
            pltpu.VMEM(wide, BF16),
            pltpu.VMEM(tall, F32),
            pltpu.VMEM(tall, F32),
            pltpu.VMEM((2, 14, slab, order), F32),
            dma((4,)),
            dma((3,)),
            dma((3,)),
            dma((2, 15)),
            dma((2, 16)),
            dma((2, 16)),
            dma((2, 16)),
            dma((2, 15)),
            dma((2, 15)),
        ],
        compiler_params=pltpu.CompilerParams(
            collective_id=0, has_side_effects=True, vmem_limit_bytes=60 * 1024 * 1024
        ),
        cost_estimate=pl.CostEstimate(flops=19 * 10**9, bytes_accessed=16 * 10**6, transcendentals=10**6),
    )(inputs, first_factor, second_factor, cotangent)


def solution(mesh):
    placed = (P("tok", "blk"), P("blk", "tok", None), P("blk", "tok", None), P("tok", "blk"))
    return jax.shard_map(
        body,
        mesh=mesh,
        in_specs=placed,
        out_specs=(P("tok", "blk"), P("blk", "tok", None), P("blk", "tok", None)),
        check_vma=False,
    )
```

```python
import math

import jax
import jax.numpy as jnp
from jax import lax
from jax.experimental import pallas as pl
from jax.experimental.pallas import tpu as pltpu
from jax.sharding import PartitionSpec as P

F32 = jnp.float32
BF16 = jnp.bfloat16
XS = 4
NN = (((1,), (0,)), ((), ()))
NT = (((1,), (1,)), ((), ()))
AG_OVER_Y = (True, False)
RS_OVER_Y = (True, False)
CUTS = 2


def halves(v):
    high = v.astype(BF16)
    return high, (v - high.astype(F32)).astype(BF16)


def product(ah, al, bh, bl, dims):
    def dot(a, b):
        return lax.dot_general(a, b, dims, preferred_element_type=F32)

    return dot(ah, bh) + (dot(ah, bl) + dot(al, bh))


def rows_at(index, size):
    return pl.ds(pl.multiple_of(index * size, size), size)


def kernel(
    x_hbm, w1_hbm, w2_hbm, cot_hbm, dx_hbm, g1_hbm, g2_hbm,
    wbuf, wh, wl, xs, cs, ah, al, xth, xtl, ft, mt, mth, mtl, d2h, d2l, dmt, d1t, rbuf,
    loc_sem, pair_send, pair_recv, ag_send, ag_recv, a2a_send, a2a_recv, rs_send, rs_recv,
):
    w_hbm = (w1_hbm, w2_hbm)
    g_hbm = (g1_hbm, g2_hbm)
    k = lax.axis_index("blk")
    t = lax.axis_index("tok")
    x = t // 4
    y = (t // 2) % 2
    c = t % 2
    oc = 1 - c
    count = x_hbm.shape[0]
    slab = w1_hbm.shape[1]
    order = w1_hbm.shape[2]
    chip = 2 * count
    group = order // 16

    def tok(dx, other_y, core):
        yy = 1 - y if other_y else y
        return {"tok": ((x + dx) % XS) * 4 + yy * 2 + core}

    def slab_of(dx, other_y, core):
        return tok(dx, other_y, core)["tok"]

    def remote(src, dst, send, recv, to):
        return pltpu.make_async_remote_copy(
            src_ref=src, dst_ref=dst, send_sem=send, recv_sem=recv, device_id=to, device_id_type=pl.DeviceIdType.MESH
        )

    mine = rows_at(c, order)
    theirs = rows_at(oc, order)
    own = rows_at(c, count)
    local = [
        pltpu.make_async_copy(x_hbm.at[:, mine], xs.at[own], loc_sem.at[0]),
        pltpu.make_async_copy(cot_hbm.at[:, mine], cs.at[own], loc_sem.at[1]),
        pltpu.make_async_copy(w1_hbm.at[c], wbuf.at[0, rows_at(t, slab)], loc_sem.at[2]),
        pltpu.make_async_copy(w2_hbm.at[c], wbuf.at[1, rows_at(t, slab)], loc_sem.at[3]),
    ]
    for cp in local:
        cp.start()

    barrier = pltpu.get_barrier_semaphore()
    near = [tok(1, False, c), tok(-1 + XS, False, c), tok(0, True, c), tok(0, False, oc)]
    near += [tok(1, False, oc), tok(-1 + XS, False, oc), tok(0, True, oc)]
    for to in near:
        pl.semaphore_signal(barrier, inc=1, device_id=to, device_id_type=pl.DeviceIdType.MESH)

    def greet(i, _):
        kk = (k + 1 + i // 2) % 8
        pl.semaphore_signal(
            barrier, inc=1, device_id={"blk": kk, "tok": t - c + i % 2}, device_id_type=pl.DeviceIdType.MESH
        )
        return 0

    lax.fori_loop(0, 14, greet, 0)
    pl.semaphore_wait(barrier, 14 + len(near))

    cut = slab // CUTS

    def piece(row, j):
        return pl.ds(pl.multiple_of(row * slab + j * cut, cut), cut)

    def ag(f, n, j, src, row, to):
        return remote(src, wbuf.at[f, piece(row, j)], ag_send.at[f, n, j], ag_recv.at[f, row, j], to)

    def forward(f, n, j, row, to):
        ag(f, n, j, wbuf.at[f, piece(row, j)], row, to).start()

    def ag_first(f):
        for j in range(CUTS):
            part = pl.ds(j * cut, cut)
            for h in range(2):
                src = w_hbm[f].at[h, part]
                ag(f, h, j, src, t, tok(1, False, h)).start()
                ag(f, 2 + h, j, src, t, tok(XS - 1, False, h)).start()
                ag(f, 4 + h, j, src, t, tok(0, True, h)).start()
            ag(f, 6, j, w_hbm[f].at[oc, part], t, tok(0, False, oc)).start()

    def ag_wait(f, row, j):
        ag(f, 0, j, wbuf.at[f, piece(row, j)], row, tok(1, False, c)).wait_recv()

    def ag_second(f):
        low, high = slab_of(XS - 1, False, 0), slab_of(1, False, 1)
        for j in range(CUTS):
            ag_wait(f, low, j)
            forward(f, 7, j, low, tok(1, False, c))
            ag_wait(f, high, j)
            forward(f, 8, j, high, tok(XS - 1, False, c))
            for h in range(2):
                row = slab_of(0, True, h)
                ag_wait(f, row, j)
                forward(f, 9 + h, j, row, tok(1, False, c))
                forward(f, 11 + h, j, row, tok(XS - 1, False, c))

    def ag_third(f):
        for j in range(CUTS):
            if AG_OVER_Y[f]:
                for h in range(2):
                    row = slab_of(2, False, h)
                    ag_wait(f, row, j)
                    forward(f, 13 + h, j, row, tok(0, True, c))
            else:
                low, high = slab_of(XS - 1, True, 0), slab_of(1, True, 1)
                ag_wait(f, low, j)
                forward(f, 13, j, low, tok(1, False, c))
                ag_wait(f, high, j)
                forward(f, 14, j, high, tok(XS - 1, False, c))

    def ag_rest(f):
        for j in range(CUTS):
            ag_wait(f, slab_of(0, False, oc), j)
            ag_wait(f, slab_of(XS - 1, False, 1), j)
            ag_wait(f, slab_of(1, False, 0), j)
            if AG_OVER_Y[f]:
                for h in range(2):
                    ag_wait(f, slab_of(1, True, h), j)
                    ag_wait(f, slab_of(XS - 1, True, h), j)
            else:
                for h in range(2):
                    ag_wait(f, slab_of(2, False, h), j)
                ag_wait(f, slab_of(XS - 1, True, 1), j)
                ag_wait(f, slab_of(1, True, 0), j)
            for h in range(2):
                ag_wait(f, slab_of(2, True, h), j)

    def ag_sent(f):
        for j in range(CUTS):
            for n in range(15):
                ag(f, n, j, wbuf.at[f, piece(t, j)], t, tok(1, False, c)).wait_send()

    def split_factor(f):
        def step(i, _):
            at = rows_at(i, 128)
            high, low = halves(wbuf[f, at, :])
            wh[f, at, :] = high
            wl[f, at, :] = low
            return 0

        lax.fori_loop(0, order // 128, step, 0)

    ag_first(0)
    pair = tok(0, False, oc)
    swap = [
        remote(x_hbm.at[:, theirs], xs.at[own], pair_send.at[0], pair_recv.at[0], pair),
        remote(cot_hbm.at[:, theirs], cs.at[own], pair_send.at[1], pair_recv.at[1], pair),
    ]
    for cp in swap:
        cp.start()
    for cp in local:
        cp.wait()
    for cp in swap:
        cp.wait()

    def split_x(i, _):
        at = rows_at(i, 128)
        high, low = halves(xs[:, at])
        ah[:, at] = high
        al[:, at] = low
        high, low = halves(xs[:, at].T)
        xth[at, :] = high
        xtl[at, :] = low
        return 0

    lax.fori_loop(0, order // 128, split_x, 0)

    ag_second(0)
    ag_third(0)
    ag_first(1)
    ag_rest(0)
    split_factor(0)

    me = 2 * k + c
    base = t - c

    def a2a(n, src, dst, s):
        return remote(
            src.at[rows_at(s, group)], dst.at[rows_at(me, group)], a2a_send.at[n, s], a2a_recv.at[n, me],
            {"blk": s // 2, "tok": base + s % 2},
        )

    def a2a_start(n, src, dst, s):
        @pl.when(s != me)
        def _():
            a2a(n, src, dst, s).start()

        @pl.when(s == me)
        def _():
            dst[rows_at(me, group), :] = src[rows_at(me, group), :]

    def a2a_wait(n, src, dst):
        def step(s, _):
            @pl.when(s != me)
            def _():
                remote(
                    src.at[rows_at(s, group)], dst.at[rows_at(s, group)], a2a_send.at[n, s], a2a_recv.at[n, s],
                    {"blk": s // 2, "tok": base + s % 2},
                ).wait_recv()

            return 0

        lax.fori_loop(0, 16, step, 0)

    def a2a_sent(n, src, dst):
        def step(s, _):
            @pl.when(s != me)
            def _():
                a2a(n, src, dst, s).wait_send()

            return 0

        lax.fori_loop(0, 16, step, 0)

    z = k // 2

    def first_step(i, _):
        q = (z + 1 + i) % 4
        at = rows_at(q, 256)
        part = product(ah[...], al[...], wh[0, :, at], wl[0, :, at], NN)
        ft[at, :] = part.T
        for r in range(4):
            a2a_start(0, ft, mt, 4 * q + r)
        return 0

    lax.fori_loop(0, 4, first_step, 0)

    ag_second(1)
    ag_third(1)
    a2a_wait(0, ft, mt)

    def turn(src, keep):
        def step(i, _):
            at = rows_at(i, 128)
            v = src[at, :]
            if keep:
                high, low = halves(v)
                mth[at, :] = high
                mtl[at, :] = low
            high, low = halves(v.T)
            ah[:, at] = high
            al[:, at] = low
            return 0

        lax.fori_loop(0, order // 128, step, 0)

    turn(mt, True)
    ag_rest(1)
    split_factor(1)

    def second_step(i, _):
        at = rows_at(i, 256)
        v = product(ah[...], al[...], wh[1, :, at], wl[1, :, at], NN)
        cdf = 0.5 * (1.0 + lax.erf(v * (1.0 / math.sqrt(2.0))))
        density = jnp.exp(-0.5 * v * v) * (1.0 / math.sqrt(2.0 * math.pi))
        high, low = halves(cs[:, at] * (cdf + v * density))
        d2h[:, at] = high
        d2l[:, at] = low
        return 0

    lax.fori_loop(0, 4, second_step, 0)

    def mixed_step(i, _):
        q = (z + 1 + i) % 4
        at = rows_at(q, 256)
        dmt[at, :] = product(wh[1, at, :], wl[1, at, :], d2h[...], d2l[...], NT)
        for r in range(4):
            a2a_start(1, dmt, d1t, 4 * q + r)
        return 0


    def rs(f, slot, j, row, to):
        return remote(
            wbuf.at[f, piece(row, j)], rbuf.at[f, slot, pl.ds(j * cut, cut)], rs_send.at[f, slot, j],
            rs_recv.at[f, slot, j], to,
        )

    def rs_start(f, slot, j, row):
        if slot >= 12 or (RS_OVER_Y[f] and slot < 2):
            to = tok(0, True, c)
        elif slot in (1, 2, 3, 7, 8, 9):
            to = tok(1, False, c)
        else:
            to = tok(XS - 1, False, c)
        rs(f, slot, j, row, to).start()

    def rs_add(f, row, j, slots):
        for slot in slots:
            rs(f, slot, j, t, tok(1, False, c)).wait_recv()
        at = piece(row, j)
        here = pl.ds(j * cut, cut)
        total = rbuf[f, slots[0], here]
        for slot in slots[1:]:
            total = total + rbuf[f, slot, here]
        wbuf[f, at, :] = wbuf[f, at, :] + total

    def gradient(f, dx, lh, ll, rh, rl):
        at = rows_at((x + dx) % XS, 256)
        wbuf[f, at, :] = product(lh[at, :], ll[at, :], rh[...], rl[...], NN)
        over_y = RS_OVER_Y[f]
        if dx == 2:
            sends = [(0, True, 0), (1, True, 1)]
            if not over_y:
                sends += [(6, False, 0), (7, False, 1)]
        elif dx == 1:
            sends = [(2, True, 0)] + ([(3, True, 1)] if over_y else []) + [(8, False, 0)]
        elif dx == 3:
            sends = [(5, True, 1)] + ([(4, True, 0)] if over_y else []) + [(11, False, 1)]
        else:
            sends = []
        for slot, other, h in sends:
            for j in range(CUTS):
                rs_start(f, slot, j, slab_of(dx, other, h))

    def rs_pass(f, j, row, slots, slot):
        rs_add(f, row, j, slots)
        rs_start(f, slot, j, row)

    def rs_middle(f):
        cuts = range(CUTS)
        if RS_OVER_Y[f]:
            for j in cuts:
                for h in range(2):
                    rs_pass(f, j, slab_of(2, False, h), (h,), 6 + h)
            for j in cuts:
                for h in range(2):
                    rs_pass(f, j, slab_of(0, True, h), (2 + h, 4 + h), 12 + h)
            for j in cuts:
                rs_pass(f, j, slab_of(1, False, 1), (7,), 9)
                rs_pass(f, j, slab_of(3, False, 0), (6,), 10)
        else:
            for j in cuts:
                rs_pass(f, j, slab_of(1, True, 1), (1,), 3)
                rs_pass(f, j, slab_of(3, True, 0), (0,), 4)
            for j in cuts:
                rs_pass(f, j, slab_of(1, False, 1), (7,), 9)
                rs_pass(f, j, slab_of(3, False, 0), (6,), 10)
            for j in cuts:
                for h in range(2):
                    rs_pass(f, j, slab_of(0, True, h), (2 + h, 4 + h), 12 + h)

    def out_local(f):
        return pltpu.make_async_copy(wbuf.at[f, rows_at(t, slab)], g_hbm[f].at[c], loc_sem.at[f])

    def out_pair(f):
        return remote(
            wbuf.at[f, rows_at(base + oc, slab)], g_hbm[f].at[c], rs_send.at[f, 14, 0], rs_recv.at[f, 14, 0], pair
        )

    def out_wait(f):
        return remote(
            wbuf.at[f, rows_at(base + oc, slab)], g_hbm[f].at[oc], rs_send.at[f, 14, 0], rs_recv.at[f, 14, 0], pair
        )

    def rs_end(f):
        for j in range(CUTS):
            for h in range(2):
                rs_add(f, slab_of(0, False, h), j, (8 + h, 10 + h, 12 + h))
        out_pair(f).start()
        out_local(f).start()

    def rs_done(f):
        out_local(f).wait()
        out_pair(f).wait_send()
        out_wait(f).wait_recv()
        for slot in range(14):
            for j in range(CUTS):
                rs(f, slot, j, t, tok(1, False, c)).wait_send()

    ag_sent(1)
    gradient(1, 2, mth, mtl, d2h, d2l)
    lax.fori_loop(0, 4, mixed_step, 0)
    for dx in (1, 3, 0):
        gradient(1, dx, mth, mtl, d2h, d2l)
    rs_middle(1)
    a2a_wait(1, dmt, d1t)
    turn(d1t, False)
    ag_sent(0)
    for dx in (2, 1, 3, 0):
        gradient(0, dx, xth, xtl, ah, al)

    def input_step(i, _):
        at = rows_at(i, 256)
        xs[:, at] = product(ah[...], al[...], wh[0, at, :], wl[0, at, :], NT)
        return 0

    lax.fori_loop(0, 4, input_step, 0)
    dx_pair = remote(xs.at[rows_at(oc, count)], dx_hbm.at[:, mine], pair_send.at[2], pair_recv.at[2], pair)
    dx_wait = remote(xs.at[rows_at(oc, count)], dx_hbm.at[:, theirs], pair_send.at[2], pair_recv.at[2], pair)
    dx_local = pltpu.make_async_copy(xs.at[own], dx_hbm.at[:, mine], loc_sem.at[2])
    dx_pair.start()
    dx_local.start()
    rs_end(1)
    rs_middle(0)
    rs_end(0)
    dx_local.wait()
    dx_pair.wait_send()
    dx_wait.wait_recv()
    a2a_sent(0, ft, mt)
    a2a_sent(1, dmt, d1t)
    rs_done(1)
    rs_done(0)


def deliver(dx_in, g1_in, g2_in, dx_out, g1_out, g2_out, dx_held, g1_held, g2_held, in_sem, out_sem):
    part = dx_in.shape[0] // 4
    steps = [(dx_in, dx_held, dx_out, pl.ds(i * part, part)) for i in range(4)]
    steps += [(g1_in, g1_held, g1_out, i) for i in range(2)]
    steps += [(g2_in, g2_held, g2_out, i) for i in range(2)]
    copies = [
        (
            pltpu.make_async_copy(src.at[at], held.at[at], in_sem.at[n]),
            pltpu.make_async_copy(held.at[at], dst.at[at], out_sem.at[n]),
        )
        for n, (src, held, dst, at) in enumerate(steps)
    ]
    for first, _ in copies:
        first.start()
    for first, second in copies:
        first.wait()
        second.start()
    for _, second in copies:
        second.wait()


def body(inputs, first_factor, second_factor, cotangent):
    count, width = inputs.shape
    blocks, slab, order = first_factor.shape
    chip = 2 * count
    wide = (chip, order)
    tall = (order, chip)
    dma = pltpu.SemaphoreType.DMA
    found = pl.pallas_call(
        kernel,
        out_shape=(
            jax.ShapeDtypeStruct((count, width), F32),
            jax.ShapeDtypeStruct((blocks, slab, order), F32),
            jax.ShapeDtypeStruct((blocks, slab, order), F32),
        ),
        in_specs=[pl.BlockSpec(memory_space=pl.ANY)] * 4,
        out_specs=[pl.BlockSpec(memory_space=pl.ANY)] * 3,
        scratch_shapes=[
            pltpu.VMEM((2, order, order), F32),
            pltpu.VMEM((2, order, order), BF16),
            pltpu.VMEM((2, order, order), BF16),
            pltpu.VMEM(wide, F32),
            pltpu.VMEM(wide, F32),
            pltpu.VMEM(wide, BF16),
            pltpu.VMEM(wide, BF16),
            pltpu.VMEM(tall, BF16),
            pltpu.VMEM(tall, BF16),
            pltpu.VMEM(tall, F32),
            pltpu.VMEM(tall, F32),
            pltpu.VMEM(tall, BF16),
            pltpu.VMEM(tall, BF16),
            pltpu.VMEM(wide, BF16),
            pltpu.VMEM(wide, BF16),
            pltpu.VMEM(tall, F32),
            pltpu.VMEM(tall, F32),
            pltpu.VMEM((2, 14, slab, order), F32),
            dma((4,)),
            dma((3,)),
            dma((3,)),
            dma((2, 15, CUTS)),
            dma((2, 16, CUTS)),
            dma((2, 16)),
            dma((2, 16)),
            dma((2, 15, CUTS)),
            dma((2, 15, CUTS)),
        ],
        compiler_params=pltpu.CompilerParams(
            collective_id=0, has_side_effects=True, vmem_limit_bytes=60 * 1024 * 1024
        ),
        cost_estimate=pl.CostEstimate(flops=19 * 10**9, bytes_accessed=16 * 10**6, transcendentals=10**6),
    )(inputs, first_factor, second_factor, cotangent)
    return pl.pallas_call(
        deliver,
        out_shape=tuple(jax.ShapeDtypeStruct(a.shape, F32) for a in found),
        in_specs=[pl.BlockSpec(memory_space=pl.ANY)] * 3,
        out_specs=[pl.BlockSpec(memory_space=pl.ANY)] * 3,
        scratch_shapes=[pltpu.VMEM(a.shape, F32) for a in found] + [dma((8,)), dma((8,))],
        cost_estimate=pl.CostEstimate(flops=0, bytes_accessed=6 * 10**6, transcendentals=0),
    )(*found)


def solution(mesh):
    placed = (P("tok", "blk"), P("blk", "tok", None), P("blk", "tok", None), P("tok", "blk"))
    return jax.shard_map(
        body,
        mesh=mesh,
        in_specs=placed,
        out_specs=(P("tok", "blk"), P("blk", "tok", None), P("blk", "tok", None)),
        check_vma=False,
    )
```

```python
import math

import jax
import jax.numpy as jnp
from jax import lax
from jax.experimental import pallas as pl
from jax.experimental.pallas import tpu as pltpu
from jax.sharding import PartitionSpec as P

F32 = jnp.float32
BF16 = jnp.bfloat16
XS = 4
NN = (((1,), (0,)), ((), ()))
NT = (((1,), (1,)), ((), ()))
AG_OVER_Y = (True, False)
RS_OVER_Y = (True, False)
CUTS = 2


def halves(v):
    high = v.astype(BF16)
    return high, (v - high.astype(F32)).astype(BF16)


def product(ah, al, bh, bl, dims):
    def dot(a, b):
        return lax.dot_general(a, b, dims, preferred_element_type=F32)

    return dot(ah, bh) + (dot(ah, bl) + dot(al, bh))


def rows_at(index, size):
    return pl.ds(pl.multiple_of(index * size, size), size)


def kernel(
    x_hbm, w1_hbm, w2_hbm, cot_hbm, dx_hbm, g1_hbm, g2_hbm,
    wbuf, gbuf, wh, wl, xs, cs, ah, al, xth, xtl, ft, mt, mth, mtl, d2h, d2l, dmt, d1t, rbuf,
    loc_sem, out_sem, pair_send, pair_recv, ag_send, ag_recv, a2a_send, a2a_recv, rs_send, rs_recv,
):
    w_hbm = (w1_hbm, w2_hbm)
    g_hbm = (g1_hbm, g2_hbm)
    k = lax.axis_index("blk")
    t = lax.axis_index("tok")
    x = t // 4
    y = (t // 2) % 2
    c = t % 2
    oc = 1 - c
    count = x_hbm.shape[0]
    slab = w1_hbm.shape[1]
    order = w1_hbm.shape[2]
    chip = 2 * count
    group = order // 16

    def tok(dx, other_y, core):
        yy = 1 - y if other_y else y
        return {"tok": ((x + dx) % XS) * 4 + yy * 2 + core}

    def slab_of(dx, other_y, core):
        return tok(dx, other_y, core)["tok"]

    def remote(src, dst, send, recv, to):
        return pltpu.make_async_remote_copy(
            src_ref=src, dst_ref=dst, send_sem=send, recv_sem=recv, device_id=to, device_id_type=pl.DeviceIdType.MESH
        )

    mine = rows_at(c, order)
    theirs = rows_at(oc, order)
    own = rows_at(c, count)
    local = [
        pltpu.make_async_copy(x_hbm.at[:, mine], xs.at[own], loc_sem.at[0]),
        pltpu.make_async_copy(cot_hbm.at[:, mine], cs.at[own], loc_sem.at[1]),
        pltpu.make_async_copy(w1_hbm.at[c], wbuf.at[0, rows_at(t, slab)], loc_sem.at[2]),
        pltpu.make_async_copy(w2_hbm.at[c], wbuf.at[1, rows_at(t, slab)], loc_sem.at[3]),
    ]
    for cp in local:
        cp.start()

    barrier = pltpu.get_barrier_semaphore()
    near = [tok(1, False, c), tok(-1 + XS, False, c), tok(0, True, c), tok(0, False, oc)]
    near += [tok(1, False, oc), tok(-1 + XS, False, oc), tok(0, True, oc)]
    for to in near:
        pl.semaphore_signal(barrier, inc=1, device_id=to, device_id_type=pl.DeviceIdType.MESH)

    def greet(i, _):
        kk = (k + 1 + i // 2) % 8
        pl.semaphore_signal(
            barrier, inc=1, device_id={"blk": kk, "tok": t - c + i % 2}, device_id_type=pl.DeviceIdType.MESH
        )
        return 0

    lax.fori_loop(0, 14, greet, 0)
    pl.semaphore_wait(barrier, 14 + len(near))

    z = k // 2
    near_half = z // 2
    wide = order // 2

    def half_of(f, j):
        if f == 0:
            return near_half if j else 1 - near_half
        return j

    def columns(f, j):
        return rows_at(half_of(f, j), wide)

    def ag(f, n, j, src, row, to):
        dst = wbuf.at[f, rows_at(row, slab), columns(f, j)]
        return remote(src, dst, ag_send.at[f, n, j], ag_recv.at[f, row, j], to)

    def forward(f, n, j, row, to):
        ag(f, n, j, wbuf.at[f, rows_at(row, slab), columns(f, j)], row, to).start()

    def ag_first(f, j):
        for h in range(2):
            src = w_hbm[f].at[h, :, columns(f, j)]
            ag(f, h, j, src, t, tok(1, False, h)).start()
            ag(f, 2 + h, j, src, t, tok(XS - 1, False, h)).start()
            ag(f, 4 + h, j, src, t, tok(0, True, h)).start()
        ag(f, 6, j, w_hbm[f].at[oc, :, columns(f, j)], t, tok(0, False, oc)).start()

    def ag_wait(f, row, j):
        ag(f, 0, j, wbuf.at[f, rows_at(row, slab), columns(f, j)], row, tok(1, False, c)).wait_recv()

    def ag_second(f, j):
        low, high = slab_of(XS - 1, False, 0), slab_of(1, False, 1)
        ag_wait(f, low, j)
        forward(f, 7, j, low, tok(1, False, c))
        ag_wait(f, high, j)
        forward(f, 8, j, high, tok(XS - 1, False, c))
        for h in range(2):
            row = slab_of(0, True, h)
            ag_wait(f, row, j)
            forward(f, 9 + h, j, row, tok(1, False, c))
            forward(f, 11 + h, j, row, tok(XS - 1, False, c))

    def ag_third(f, j):
        if AG_OVER_Y[f]:
            for h in range(2):
                row = slab_of(2, False, h)
                ag_wait(f, row, j)
                forward(f, 13 + h, j, row, tok(0, True, c))
        else:
            low, high = slab_of(XS - 1, True, 0), slab_of(1, True, 1)
            ag_wait(f, low, j)
            forward(f, 13, j, low, tok(1, False, c))
            ag_wait(f, high, j)
            forward(f, 14, j, high, tok(XS - 1, False, c))

    def ag_rest(f, j):
        ag_wait(f, slab_of(0, False, oc), j)
        ag_wait(f, slab_of(XS - 1, False, 1), j)
        ag_wait(f, slab_of(1, False, 0), j)
        if AG_OVER_Y[f]:
            for h in range(2):
                ag_wait(f, slab_of(1, True, h), j)
                ag_wait(f, slab_of(XS - 1, True, h), j)
        else:
            for h in range(2):
                ag_wait(f, slab_of(2, False, h), j)
            ag_wait(f, slab_of(XS - 1, True, 1), j)
            ag_wait(f, slab_of(1, True, 0), j)
        for h in range(2):
            ag_wait(f, slab_of(2, True, h), j)

    def ag_sent(f, j):
        for n in range(15):
            ag(f, n, j, wbuf.at[f, rows_at(t, slab), columns(f, j)], t, tok(1, False, c)).wait_send()

    def split_factor(f, j):
        across = columns(f, j)

        def step(i, _):
            at = rows_at(i, 128)
            high, low = halves(wbuf[f, at, across])
            wh[f, at, across] = high
            wl[f, at, across] = low
            return 0

        lax.fori_loop(0, order // 128, step, 0)

    ag_first(0, 0)
    ag_first(0, 1)
    pair = tok(0, False, oc)
    swap = [
        remote(x_hbm.at[:, theirs], xs.at[own], pair_send.at[0], pair_recv.at[0], pair),
        remote(cot_hbm.at[:, theirs], cs.at[own], pair_send.at[1], pair_recv.at[1], pair),
    ]
    for cp in swap:
        cp.start()
    for cp in local:
        cp.wait()
    for cp in swap:
        cp.wait()

    def split_x(i, _):
        at = rows_at(i, 128)
        high, low = halves(xs[:, at])
        ah[:, at] = high
        al[:, at] = low
        high, low = halves(xs[:, at].T)
        xth[at, :] = high
        xtl[at, :] = low
        return 0

    lax.fori_loop(0, order // 128, split_x, 0)

    me = 2 * k + c
    base = t - c

    def a2a(n, src, dst, s):
        return remote(
            src.at[rows_at(s, group)], dst.at[rows_at(me, group)], a2a_send.at[n, s], a2a_recv.at[n, me],
            {"blk": s // 2, "tok": base + s % 2},
        )

    def a2a_start(n, src, dst, s):
        @pl.when(s != me)
        def _():
            a2a(n, src, dst, s).start()

        @pl.when(s == me)
        def _():
            dst[rows_at(me, group), :] = src[rows_at(me, group), :]

    def a2a_wait(n, src, dst, half):
        def step(i, _):
            s = 8 * half + i

            @pl.when(s != me)
            def _():
                remote(
                    src.at[rows_at(s, group)], dst.at[rows_at(s, group)], a2a_send.at[n, s], a2a_recv.at[n, s],
                    {"blk": s // 2, "tok": base + s % 2},
                ).wait_recv()

            return 0

        lax.fori_loop(0, 8, step, 0)

    def a2a_sent(n, src, dst):
        def step(s, _):
            @pl.when(s != me)
            def _():
                a2a(n, src, dst, s).wait_send()

            return 0

        lax.fori_loop(0, 16, step, 0)

    def turn(src, half, keep):
        def step(i, _):
            at = rows_at(half * 4 + i, 128)
            v = src[at, :]
            if keep:
                high, low = halves(v)
                mth[at, :] = high
                mtl[at, :] = low
            high, low = halves(v.T)
            ah[:, at] = high
            al[:, at] = low
            return 0

        lax.fori_loop(0, 4, step, 0)

    def quarter(i):
        if i < 2:
            return 2 * (1 - near_half) + (z + i) % 2
        return 2 * near_half + (z + i + 1) % 2

    def first(j):
        for i in (2 * j, 2 * j + 1):
            q = quarter(i)
            at = rows_at(q, 256)
            part = product(ah[...], al[...], wh[0, :, at], wl[0, :, at], NN)
            ft[at, :] = part.T
            for r in range(4):
                a2a_start(0, ft, mt, 4 * q + r)

    def second(j):
        def step(i, _):
            at = rows_at(2 * j + i, 256)
            v = product(ah[...], al[...], wh[1, :, at], wl[1, :, at], NN)
            cdf = 0.5 * (1.0 + lax.erf(v * (1.0 / math.sqrt(2.0))))
            density = jnp.exp(-0.5 * v * v) * (1.0 / math.sqrt(2.0 * math.pi))
            high, low = halves(cs[:, at] * (cdf + v * density))
            d2h[:, at] = high
            d2l[:, at] = low
            return 0

        lax.fori_loop(0, 2, step, 0)

    def back():
        for i in range(4):
            q = quarter(i)
            at = rows_at(q, 256)
            dmt[at, :] = product(wh[1, at, :], wl[1, at, :], d2h[...], d2l[...], NT)
            for r in range(4):
                a2a_start(1, dmt, d1t, 4 * q + r)

    def rs(f, slot, j, row, to):
        return remote(
            gbuf.at[f, rows_at(row, slab), columns(f, j)], rbuf.at[f, slot, :, pl.ds(j * wide, wide)],
            rs_send.at[f, slot, j], rs_recv.at[f, slot, j], to,
        )

    def rs_start(f, slot, j, row):
        if slot >= 12 or (RS_OVER_Y[f] and slot < 2):
            to = tok(0, True, c)
        elif slot in (1, 2, 3, 7, 8, 9):
            to = tok(1, False, c)
        else:
            to = tok(XS - 1, False, c)
        rs(f, slot, j, row, to).start()

    def rs_add(f, row, j, slots):
        for slot in slots:
            rs(f, slot, j, t, tok(1, False, c)).wait_recv()
        at = rows_at(row, slab)
        across = columns(f, j)
        here = pl.ds(j * wide, wide)
        total = rbuf[f, slots[0], :, here]
        for slot in slots[1:]:
            total = total + rbuf[f, slot, :, here]
        gbuf[f, at, across] = gbuf[f, at, across] + total

    def gradient(f, j, dx, lh, ll, rh, rl):
        at = rows_at((x + dx) % XS, 256)
        across = columns(f, j)
        gbuf[f, at, across] = product(lh[at, :], ll[at, :], rh[:, across], rl[:, across], NN)
        over_y = RS_OVER_Y[f]
        if dx == 2:
            sends = [(0, True, 0), (1, True, 1)]
            if not over_y:
                sends += [(6, False, 0), (7, False, 1)]
        elif dx == 1:
            sends = [(2, True, 0)] + ([(3, True, 1)] if over_y else []) + [(8, False, 0)]
        elif dx == 3:
            sends = [(5, True, 1)] + ([(4, True, 0)] if over_y else []) + [(11, False, 1)]
        else:
            sends = []
        for slot, other, h in sends:
            rs_start(f, slot, j, slab_of(dx, other, h))

    def rs_pass(f, j, row, slots, slot):
        rs_add(f, row, j, slots)
        rs_start(f, slot, j, row)

    def rs_far(f, j):
        if RS_OVER_Y[f]:
            for h in range(2):
                rs_pass(f, j, slab_of(2, False, h), (h,), 6 + h)
        else:
            rs_pass(f, j, slab_of(1, True, 1), (1,), 3)
            rs_pass(f, j, slab_of(3, True, 0), (0,), 4)

    def rs_along(f, j):
        rs_pass(f, j, slab_of(1, False, 1), (7,), 9)
        rs_pass(f, j, slab_of(3, False, 0), (6,), 10)

    def rs_across(f, j):
        for h in range(2):
            rs_pass(f, j, slab_of(0, True, h), (2 + h, 4 + h), 12 + h)

    def out_local(f, j):
        across = columns(f, j)
        return pltpu.make_async_copy(
            gbuf.at[f, rows_at(t, slab), across], g_hbm[f].at[c, :, across], out_sem.at[f, j]
        )

    def out_pair(f, j, block):
        across = columns(f, j)
        return remote(
            gbuf.at[f, rows_at(base + oc, slab), across], g_hbm[f].at[block, :, across],
            rs_send.at[f, 14, j], rs_recv.at[f, 14, j], pair,
        )

    def rs_end(f, j):
        for h in range(2):
            rs_add(f, slab_of(0, False, h), j, (8 + h, 10 + h, 12 + h))
        out_pair(f, j, c).start()
        out_local(f, j).start()

    def rs_done(f, j):
        out_local(f, j).wait()
        out_pair(f, j, c).wait_send()
        out_pair(f, j, oc).wait_recv()
        for slot in range(14):
            rs(f, slot, j, t, tok(1, False, c)).wait_send()

    ag_second(0, 0)
    ag_third(0, 0)
    ag_second(0, 1)
    ag_first(1, 0)
    ag_rest(0, 0)
    split_factor(0, 0)
    first(0)
    ag_third(0, 1)
    ag_second(1, 0)
    ag_first(1, 1)
    ag_rest(0, 1)
    split_factor(0, 1)
    first(1)
    ag_third(1, 0)
    ag_second(1, 1)
    ag_rest(1, 0)
    split_factor(1, 0)
    for half in (1 - near_half, near_half):
        a2a_wait(0, ft, mt, half)
        turn(mt, half, True)
    ag_third(1, 1)
    second(0)
    for dx in (2, 1, 3, 0):
        gradient(1, 0, dx, mth, mtl, d2h, d2l)
    ag_rest(1, 1)
    split_factor(1, 1)
    second(1)
    gradient(1, 1, 2, mth, mtl, d2h, d2l)
    back()
    for dx in (1, 3, 0):
        gradient(1, 1, dx, mth, mtl, d2h, d2l)
    rs_far(1, 0)
    rs_along(1, 0)
    rs_far(1, 1)
    rs_along(1, 1)
    rs_across(1, 0)
    a2a_wait(1, dmt, d1t, 1 - near_half)
    turn(d1t, 1 - near_half, False)
    for dx in (2, 1, 3, 0):
        gradient(0, 0, dx, xth, xtl, ah, al)
    rs_across(1, 1)
    a2a_wait(1, dmt, d1t, near_half)
    turn(d1t, near_half, False)
    for dx in (2, 1, 3, 0):
        gradient(0, 1, dx, xth, xtl, ah, al)

    def input_step(i, _):
        at = rows_at(i, 256)
        xs[:, at] = product(ah[...], al[...], wh[0, at, :], wl[0, at, :], NT)
        return 0

    lax.fori_loop(0, 4, input_step, 0)
    dx_pair = remote(xs.at[rows_at(oc, count)], dx_hbm.at[:, mine], pair_send.at[2], pair_recv.at[2], pair)
    dx_wait = remote(xs.at[rows_at(oc, count)], dx_hbm.at[:, theirs], pair_send.at[2], pair_recv.at[2], pair)
    dx_local = pltpu.make_async_copy(xs.at[own], dx_hbm.at[:, mine], loc_sem.at[2])
    dx_pair.start()
    dx_local.start()
    rs_far(0, 0)
    rs_across(0, 0)
    rs_far(0, 1)
    rs_along(0, 0)
    rs_across(0, 1)
    rs_end(1, 0)
    rs_along(0, 1)
    rs_end(1, 1)
    rs_end(0, 0)
    rs_end(0, 1)
    dx_local.wait()
    dx_pair.wait_send()
    dx_wait.wait_recv()
    a2a_sent(0, ft, mt)
    a2a_sent(1, dmt, d1t)
    for f in range(2):
        for j in range(CUTS):
            ag_sent(f, j)
            rs_done(f, j)


def deliver(dx_in, g1_in, g2_in, dx_out, g1_out, g2_out, dx_held, g1_held, g2_held, in_sem, out_sem):
    part = dx_in.shape[0] // 4
    steps = [(dx_in, dx_held, dx_out, pl.ds(i * part, part)) for i in range(4)]
    steps += [(g1_in, g1_held, g1_out, i) for i in range(2)]
    steps += [(g2_in, g2_held, g2_out, i) for i in range(2)]
    copies = [
        (
            pltpu.make_async_copy(src.at[at], held.at[at], in_sem.at[n]),
            pltpu.make_async_copy(held.at[at], dst.at[at], out_sem.at[n]),
        )
        for n, (src, held, dst, at) in enumerate(steps)
    ]
    for first, _ in copies:
        first.start()
    for first, second in copies:
        first.wait()
        second.start()
    for _, second in copies:
        second.wait()


def body(inputs, first_factor, second_factor, cotangent):
    count, width = inputs.shape
    blocks, slab, order = first_factor.shape
    chip = 2 * count
    wide = (chip, order)
    tall = (order, chip)
    dma = pltpu.SemaphoreType.DMA
    found = pl.pallas_call(
        kernel,
        out_shape=(
            jax.ShapeDtypeStruct((count, width), F32),
            jax.ShapeDtypeStruct((blocks, slab, order), F32),
            jax.ShapeDtypeStruct((blocks, slab, order), F32),
        ),
        in_specs=[pl.BlockSpec(memory_space=pl.ANY)] * 4,
        out_specs=[pl.BlockSpec(memory_space=pl.ANY)] * 3,
        scratch_shapes=[
            pltpu.VMEM((2, order, order), F32),
            pltpu.VMEM((2, order, order), F32),
            pltpu.VMEM((2, order, order), BF16),
            pltpu.VMEM((2, order, order), BF16),
            pltpu.VMEM(wide, F32),
            pltpu.VMEM(wide, F32),
            pltpu.VMEM(wide, BF16),
            pltpu.VMEM(wide, BF16),
            pltpu.VMEM(tall, BF16),
            pltpu.VMEM(tall, BF16),
            pltpu.VMEM(tall, F32),
            pltpu.VMEM(tall, F32),
            pltpu.VMEM(tall, BF16),
            pltpu.VMEM(tall, BF16),
            pltpu.VMEM(wide, BF16),
            pltpu.VMEM(wide, BF16),
            pltpu.VMEM(tall, F32),
            pltpu.VMEM(tall, F32),
            pltpu.VMEM((2, 14, slab, order), F32),
            dma((4,)),
            dma((2, CUTS)),
            dma((3,)),
            dma((3,)),
            dma((2, 15, CUTS)),
            dma((2, 16, CUTS)),
            dma((2, 16)),
            dma((2, 16)),
            dma((2, 15, CUTS)),
            dma((2, 15, CUTS)),
        ],
        compiler_params=pltpu.CompilerParams(
            collective_id=0, has_side_effects=True, vmem_limit_bytes=60 * 1024 * 1024
        ),
        cost_estimate=pl.CostEstimate(flops=19 * 10**9, bytes_accessed=16 * 10**6, transcendentals=10**6),
    )(inputs, first_factor, second_factor, cotangent)
    return pl.pallas_call(
        deliver,
        out_shape=tuple(jax.ShapeDtypeStruct(a.shape, F32) for a in found),
        in_specs=[pl.BlockSpec(memory_space=pl.ANY)] * 3,
        out_specs=[pl.BlockSpec(memory_space=pl.ANY)] * 3,
        scratch_shapes=[pltpu.VMEM(a.shape, F32) for a in found] + [dma((8,)), dma((8,))],
        cost_estimate=pl.CostEstimate(flops=0, bytes_accessed=6 * 10**6, transcendentals=0),
    )(*found)


def solution(mesh):
    placed = (P("tok", "blk"), P("blk", "tok", None), P("blk", "tok", None), P("tok", "blk"))
    return jax.shard_map(
        body,
        mesh=mesh,
        in_specs=placed,
        out_specs=(P("tok", "blk"), P("blk", "tok", None), P("blk", "tok", None)),
        check_vma=False,
    )
```

```python
import math

import jax
import jax.numpy as jnp
from jax import lax
from jax.experimental import pallas as pl
from jax.experimental.pallas import tpu as pltpu
from jax.sharding import PartitionSpec as P

F32 = jnp.float32
BF16 = jnp.bfloat16
XS = 4
NN = (((1,), (0,)), ((), ()))
NT = (((1,), (1,)), ((), ()))
AG_OVER_Y = ((True, False), (False, False))
RS_OVER_Y = (True, False)
CUTS = 2


def halves(v):
    high = v.astype(BF16)
    return high, (v - high.astype(F32)).astype(BF16)


def product(ah, al, bh, bl, dims):
    def dot(a, b):
        return lax.dot_general(a, b, dims, preferred_element_type=F32)

    return dot(ah, bh) + (dot(ah, bl) + dot(al, bh))


def rows_at(index, size):
    return pl.ds(pl.multiple_of(index * size, size), size)


def kernel(
    x_hbm, w1_hbm, w2_hbm, cot_hbm, dx_hbm, g1_hbm, g2_hbm,
    wbuf, gbuf, wh, wl, xs, cs, ah, al, xth, xtl, ft, mt, mth, mtl, d2h, d2l, dmt, d1t, rbuf,
    loc_sem, out_sem, pair_send, pair_recv, ag_send, ag_recv, a2a_send, a2a_recv, rs_send, rs_recv,
):
    w_hbm = (w1_hbm, w2_hbm)
    g_hbm = (g1_hbm, g2_hbm)
    k = lax.axis_index("blk")
    t = lax.axis_index("tok")
    x = t // 4
    y = (t // 2) % 2
    c = t % 2
    oc = 1 - c
    count = x_hbm.shape[0]
    slab = w1_hbm.shape[1]
    order = w1_hbm.shape[2]
    chip = 2 * count
    group = order // 16

    def tok(dx, other_y, core):
        yy = 1 - y if other_y else y
        return {"tok": ((x + dx) % XS) * 4 + yy * 2 + core}

    def slab_of(dx, other_y, core):
        return tok(dx, other_y, core)["tok"]

    def remote(src, dst, send, recv, to):
        return pltpu.make_async_remote_copy(
            src_ref=src, dst_ref=dst, send_sem=send, recv_sem=recv, device_id=to, device_id_type=pl.DeviceIdType.MESH
        )

    mine = rows_at(c, order)
    theirs = rows_at(oc, order)
    own = rows_at(c, count)
    local = [
        pltpu.make_async_copy(x_hbm.at[:, mine], xs.at[own], loc_sem.at[0]),
        pltpu.make_async_copy(cot_hbm.at[:, mine], cs.at[own], loc_sem.at[1]),
        pltpu.make_async_copy(w1_hbm.at[c], wbuf.at[0, rows_at(t, slab)], loc_sem.at[2]),
        pltpu.make_async_copy(w2_hbm.at[c], wbuf.at[1, rows_at(t, slab)], loc_sem.at[3]),
    ]
    for cp in local:
        cp.start()

    barrier = pltpu.get_barrier_semaphore()
    near = [tok(1, False, c), tok(-1 + XS, False, c), tok(0, True, c), tok(0, False, oc)]
    near += [tok(1, False, oc), tok(-1 + XS, False, oc), tok(0, True, oc)]
    for to in near:
        pl.semaphore_signal(barrier, inc=1, device_id=to, device_id_type=pl.DeviceIdType.MESH)

    def greet(i, _):
        kk = (k + 1 + i // 2) % 8
        pl.semaphore_signal(
            barrier, inc=1, device_id={"blk": kk, "tok": t - c + i % 2}, device_id_type=pl.DeviceIdType.MESH
        )
        return 0

    lax.fori_loop(0, 14, greet, 0)
    pl.semaphore_wait(barrier, 14 + len(near))

    z = k // 2
    near_half = z // 2
    wide = order // 2

    def half_of(f, j):
        if f == 0:
            return near_half if j else 1 - near_half
        return j

    def columns(f, j):
        return rows_at(half_of(f, j), wide)

    def ag(f, n, j, src, row, to):
        dst = wbuf.at[f, rows_at(row, slab), columns(f, j)]
        return remote(src, dst, ag_send.at[f, n, j], ag_recv.at[f, row, j], to)

    def forward(f, n, j, row, to):
        ag(f, n, j, wbuf.at[f, rows_at(row, slab), columns(f, j)], row, to).start()

    def ag_first(f, j):
        for h in range(2):
            src = w_hbm[f].at[h, :, columns(f, j)]
            ag(f, h, j, src, t, tok(1, False, h)).start()
            ag(f, 2 + h, j, src, t, tok(XS - 1, False, h)).start()
            ag(f, 4 + h, j, src, t, tok(0, True, h)).start()
        ag(f, 6, j, w_hbm[f].at[oc, :, columns(f, j)], t, tok(0, False, oc)).start()

    def ag_wait(f, row, j):
        ag(f, 0, j, wbuf.at[f, rows_at(row, slab), columns(f, j)], row, tok(1, False, c)).wait_recv()

    def ag_second(f, j):
        low, high = slab_of(XS - 1, False, 0), slab_of(1, False, 1)
        ag_wait(f, low, j)
        forward(f, 7, j, low, tok(1, False, c))
        ag_wait(f, high, j)
        forward(f, 8, j, high, tok(XS - 1, False, c))
        for h in range(2):
            row = slab_of(0, True, h)
            ag_wait(f, row, j)
            forward(f, 9 + h, j, row, tok(1, False, c))
            forward(f, 11 + h, j, row, tok(XS - 1, False, c))

    def ag_third(f, j):
        if AG_OVER_Y[f][j]:
            for h in range(2):
                row = slab_of(2, False, h)
                ag_wait(f, row, j)
                forward(f, 13 + h, j, row, tok(0, True, c))
        else:
            low, high = slab_of(XS - 1, True, 0), slab_of(1, True, 1)
            ag_wait(f, low, j)
            forward(f, 13, j, low, tok(1, False, c))
            ag_wait(f, high, j)
            forward(f, 14, j, high, tok(XS - 1, False, c))

    def ag_rest(f, j):
        ag_wait(f, slab_of(0, False, oc), j)
        ag_wait(f, slab_of(XS - 1, False, 1), j)
        ag_wait(f, slab_of(1, False, 0), j)
        if AG_OVER_Y[f][j]:
            for h in range(2):
                ag_wait(f, slab_of(1, True, h), j)
                ag_wait(f, slab_of(XS - 1, True, h), j)
        else:
            for h in range(2):
                ag_wait(f, slab_of(2, False, h), j)
            ag_wait(f, slab_of(XS - 1, True, 1), j)
            ag_wait(f, slab_of(1, True, 0), j)
        for h in range(2):
            ag_wait(f, slab_of(2, True, h), j)

    def ag_sent(f, j):
        for n in range(15):
            ag(f, n, j, wbuf.at[f, rows_at(t, slab), columns(f, j)], t, tok(1, False, c)).wait_send()

    def split_factor(f, j):
        across = columns(f, j)

        def step(i, _):
            at = rows_at(i, 128)
            high, low = halves(wbuf[f, at, across])
            wh[f, at, across] = high
            wl[f, at, across] = low
            return 0

        lax.fori_loop(0, order // 128, step, 0)

    pair = tok(0, False, oc)
    swap = [
        remote(x_hbm.at[:, theirs], xs.at[own], pair_send.at[0], pair_recv.at[0], pair),
        remote(cot_hbm.at[:, theirs], cs.at[own], pair_send.at[1], pair_recv.at[1], pair),
    ]
    swap[0].start()
    ag_first(0, 0)
    ag_first(0, 1)
    for cp in local:
        cp.wait()

    def split_x(i, _):
        at = rows_at(i, 128)
        high, low = halves(xs[:, at])
        ah[:, at] = high
        al[:, at] = low
        high, low = halves(xs[:, at].T)
        xth[at, :] = high
        xtl[at, :] = low
        return 0


    me = 2 * k + c
    base = t - c

    def a2a(n, src, dst, s):
        return remote(
            src.at[rows_at(s, group)], dst.at[rows_at(me, group)], a2a_send.at[n, s], a2a_recv.at[n, me],
            {"blk": s // 2, "tok": base + s % 2},
        )

    def a2a_start(n, src, dst, s):
        @pl.when(s != me)
        def _():
            a2a(n, src, dst, s).start()

        @pl.when(s == me)
        def _():
            dst[rows_at(me, group), :] = src[rows_at(me, group), :]

    def a2a_wait(n, src, dst, half):
        def step(i, _):
            s = 8 * half + i

            @pl.when(s != me)
            def _():
                remote(
                    src.at[rows_at(s, group)], dst.at[rows_at(s, group)], a2a_send.at[n, s], a2a_recv.at[n, s],
                    {"blk": s // 2, "tok": base + s % 2},
                ).wait_recv()

            return 0

        lax.fori_loop(0, 8, step, 0)

    def a2a_sent(n, src, dst):
        def step(s, _):
            @pl.when(s != me)
            def _():
                a2a(n, src, dst, s).wait_send()

            return 0

        lax.fori_loop(0, 16, step, 0)

    def turn(src, half, keep):
        def step(i, _):
            at = rows_at(half * 4 + i, 128)
            v = src[at, :]
            if keep:
                high, low = halves(v)
                mth[at, :] = high
                mtl[at, :] = low
            high, low = halves(v.T)
            ah[:, at] = high
            al[:, at] = low
            return 0

        lax.fori_loop(0, 4, step, 0)

    def quarter(i):
        if i < 2:
            return 2 * (1 - near_half) + (z + i) % 2
        return 2 * near_half + (z + i + 1) % 2

    def first(j):
        for i in (2 * j, 2 * j + 1):
            q = quarter(i)
            at = rows_at(q, 256)
            part = product(ah[...], al[...], wh[0, :, at], wl[0, :, at], NN)
            ft[at, :] = part.T
            for r in range(4):
                a2a_start(0, ft, mt, 4 * q + r)

    def second(j):
        def step(i, _):
            at = rows_at(2 * j + i, 256)
            v = product(ah[...], al[...], wh[1, :, at], wl[1, :, at], NN)
            cdf = 0.5 * (1.0 + lax.erf(v * (1.0 / math.sqrt(2.0))))
            density = jnp.exp(-0.5 * v * v) * (1.0 / math.sqrt(2.0 * math.pi))
            high, low = halves(cs[:, at] * (cdf + v * density))
            d2h[:, at] = high
            d2l[:, at] = low
            return 0

        lax.fori_loop(0, 2, step, 0)

    def back():
        for i in range(4):
            q = quarter(i)
            at = rows_at(q, 256)
            dmt[at, :] = product(wh[1, at, :], wl[1, at, :], d2h[...], d2l[...], NT)
            for r in range(4):
                a2a_start(1, dmt, d1t, 4 * q + r)

    def rs(f, slot, j, row, to, there=None):
        there = slot if there is None else there
        return remote(
            gbuf.at[f, rows_at(row, slab), columns(f, j)], rbuf.at[f, there, :, pl.ds(j * wide, wide)],
            rs_send.at[f, slot, j], rs_recv.at[f, there, j], to,
        )

    def rs_start(f, slot, j, row):
        core = slot % 2 if slot >= 8 else c
        there = slot - slot % 2 + c if slot >= 8 else slot
        if slot >= 12 or (RS_OVER_Y[f] and slot < 2):
            to = tok(0, True, core)
        elif slot in (1, 2, 3, 7, 8, 9):
            to = tok(1, False, core)
        else:
            to = tok(XS - 1, False, core)
        rs(f, slot, j, row, to, there).start()

    def rs_add(f, row, j, slots):
        for slot in slots:
            rs(f, slot, j, t, tok(1, False, c)).wait_recv()
        at = rows_at(row, slab)
        across = columns(f, j)
        here = pl.ds(j * wide, wide)
        total = rbuf[f, slots[0], :, here]
        for slot in slots[1:]:
            total = total + rbuf[f, slot, :, here]
        gbuf[f, at, across] = gbuf[f, at, across] + total

    def gradient(f, j, dx, lh, ll, rh, rl):
        at = rows_at((x + dx) % XS, 256)
        across = columns(f, j)
        gbuf[f, at, across] = product(lh[at, :], ll[at, :], rh[:, across], rl[:, across], NN)
        over_y = RS_OVER_Y[f]
        if dx == 2:
            sends = [(0, True, 0), (1, True, 1)]
            if not over_y:
                sends += [(6, False, 0), (7, False, 1)]
        elif dx == 1:
            sends = [(2, True, 0)] + ([(3, True, 1)] if over_y else []) + [(8, False, 0)]
        elif dx == 3:
            sends = [(5, True, 1)] + ([(4, True, 0)] if over_y else []) + [(11, False, 1)]
        else:
            sends = []
        for slot, other, h in sends:
            rs_start(f, slot, j, slab_of(dx, other, h))
        if dx == 0:
            rs(f, 14, j, slab_of(0, False, oc), pair).start()

    def rs_pass(f, j, row, slots, slot):
        rs_add(f, row, j, slots)
        rs_start(f, slot, j, row)

    def rs_far(f, j):
        if RS_OVER_Y[f]:
            for h in range(2):
                rs_pass(f, j, slab_of(2, False, h), (h,), 6 + h)
        else:
            rs_pass(f, j, slab_of(1, True, 1), (1,), 3)
            rs_pass(f, j, slab_of(3, True, 0), (0,), 4)

    def rs_along(f, j):
        rs_pass(f, j, slab_of(1, False, 1), (7,), 9)
        rs_pass(f, j, slab_of(3, False, 0), (6,), 10)

    def rs_across(f, j):
        for h in range(2):
            rs_pass(f, j, slab_of(0, True, h), (2 + h, 4 + h), 12 + h)

    def out_own(f, j):
        across = columns(f, j)
        return pltpu.make_async_copy(
            gbuf.at[f, rows_at(t, slab), across], g_hbm[f].at[c, :, across], out_sem.at[f, j, 0]
        )

    def out_other(f, j):
        return pltpu.make_async_copy(
            rbuf.at[f, 14, :, pl.ds(j * wide, wide)], g_hbm[f].at[oc, :, columns(f, j)], out_sem.at[f, j, 1]
        )

    def rs_end(f, j):
        rs_add(f, t, j, (8 + c, 10 + c, 12 + c))
        out_own(f, j).start()
        here = pl.ds(j * wide, wide)
        slots = (14, 8 + oc, 10 + oc, 12 + oc)
        for slot in slots:
            rs(f, slot, j, t, pair).wait_recv()
        total = rbuf[f, slots[0], :, here]
        for slot in slots[1:]:
            total = total + rbuf[f, slot, :, here]
        rbuf[f, 14, :, here] = total
        out_other(f, j).start()

    def rs_done(f, j):
        out_own(f, j).wait()
        out_other(f, j).wait()

    def rs_sent(f, j):
        for slot in range(15):
            rs(f, slot, j, t, tok(1, False, c)).wait_send()

    ag_second(0, 0)
    swap[1].start()
    swap[0].wait()
    lax.fori_loop(0, order // 128, split_x, 0)
    ag_third(0, 0)
    ag_second(0, 1)
    ag_first(1, 0)
    ag_rest(0, 0)
    split_factor(0, 0)
    first(0)
    ag_third(0, 1)
    ag_second(1, 0)
    ag_first(1, 1)
    ag_rest(0, 1)
    split_factor(0, 1)
    first(1)
    ag_third(1, 0)
    ag_second(1, 1)
    ag_rest(1, 0)
    split_factor(1, 0)
    for half in (1 - near_half, near_half):
        a2a_wait(0, ft, mt, half)
        turn(mt, half, True)
    ag_third(1, 1)
    swap[1].wait()
    second(0)
    for dx in (2, 1, 3):
        gradient(1, 0, dx, mth, mtl, d2h, d2l)
    ag_rest(1, 1)
    split_factor(1, 1)
    second(1)
    back()
    for dx in (2, 1, 3, 0):
        gradient(1, 1, dx, mth, mtl, d2h, d2l)
    gradient(1, 0, 0, mth, mtl, d2h, d2l)
    rs_far(1, 0)
    rs_along(1, 0)
    rs_far(1, 1)
    rs_along(1, 1)
    rs_across(1, 0)
    a2a_wait(1, dmt, d1t, 1 - near_half)
    turn(d1t, 1 - near_half, False)
    for dx in (2, 1, 3, 0):
        gradient(0, 0, dx, xth, xtl, ah, al)
    rs_across(1, 1)
    a2a_wait(1, dmt, d1t, near_half)
    turn(d1t, near_half, False)
    for dx in (2, 1, 3, 0):
        gradient(0, 1, dx, xth, xtl, ah, al)

    def input_step(i, _):
        at = rows_at(i, 256)
        xs[:, at] = product(ah[...], al[...], wh[0, at, :], wl[0, at, :], NT)
        return 0

    rs_far(0, 0)
    lax.fori_loop(0, 2, input_step, 0)
    rs_across(0, 0)
    rs_far(0, 1)
    lax.fori_loop(2, 4, input_step, 0)
    dx_pair = remote(xs.at[rows_at(oc, count)], dx_hbm.at[:, mine], pair_send.at[2], pair_recv.at[2], pair)
    dx_wait = remote(xs.at[rows_at(oc, count)], dx_hbm.at[:, theirs], pair_send.at[2], pair_recv.at[2], pair)
    dx_local = pltpu.make_async_copy(xs.at[own], dx_hbm.at[:, mine], loc_sem.at[2])
    dx_pair.start()
    dx_local.start()
    rs_along(0, 0)
    rs_across(0, 1)
    rs_end(1, 0)
    ag_sent(0, 0)
    ag_sent(0, 1)
    ag_sent(1, 0)
    ag_sent(1, 1)
    a2a_sent(0, ft, mt)
    a2a_sent(1, dmt, d1t)
    rs_end(1, 1)
    rs_sent(1, 0)
    rs_sent(1, 1)
    rs_done(1, 0)
    dx_local.wait()
    dx_pair.wait_send()
    dx_wait.wait_recv()
    rs_along(0, 1)
    rs_end(0, 0)
    rs_done(1, 1)
    rs_sent(0, 0)
    rs_end(0, 1)
    rs_sent(0, 1)
    rs_done(0, 0)
    rs_done(0, 1)


def deliver(dx_in, g1_in, g2_in, dx_out, g1_out, g2_out, dx_held, g1_held, g2_held, in_sem, out_sem):
    part = dx_in.shape[0] // 4
    steps = [(dx_in, dx_held, dx_out, pl.ds(i * part, part)) for i in range(4)]
    steps += [(g1_in, g1_held, g1_out, i) for i in range(2)]
    steps += [(g2_in, g2_held, g2_out, i) for i in range(2)]
    copies = [
        (
            pltpu.make_async_copy(src.at[at], held.at[at], in_sem.at[n]),
            pltpu.make_async_copy(held.at[at], dst.at[at], out_sem.at[n]),
        )
        for n, (src, held, dst, at) in enumerate(steps)
    ]
    for first, _ in copies:
        first.start()
    for first, second in copies:
        first.wait()
        second.start()
    for _, second in copies:
        second.wait()


def body(inputs, first_factor, second_factor, cotangent):
    count, width = inputs.shape
    blocks, slab, order = first_factor.shape
    chip = 2 * count
    wide = (chip, order)
    tall = (order, chip)
    dma = pltpu.SemaphoreType.DMA
    found = pl.pallas_call(
        kernel,
        out_shape=(
            jax.ShapeDtypeStruct((count, width), F32),
            jax.ShapeDtypeStruct((blocks, slab, order), F32),
            jax.ShapeDtypeStruct((blocks, slab, order), F32),
        ),
        in_specs=[pl.BlockSpec(memory_space=pl.ANY)] * 4,
        out_specs=[pl.BlockSpec(memory_space=pl.ANY)] * 3,
        scratch_shapes=[
            pltpu.VMEM((2, order, order), F32),
            pltpu.VMEM((2, order, order), F32),
            pltpu.VMEM((2, order, order), BF16),
            pltpu.VMEM((2, order, order), BF16),
            pltpu.VMEM(wide, F32),
            pltpu.VMEM(wide, F32),
            pltpu.VMEM(wide, BF16),
            pltpu.VMEM(wide, BF16),
            pltpu.VMEM(tall, BF16),
            pltpu.VMEM(tall, BF16),
            pltpu.VMEM(tall, F32),
            pltpu.VMEM(tall, F32),
            pltpu.VMEM(tall, BF16),
            pltpu.VMEM(tall, BF16),
            pltpu.VMEM(wide, BF16),
            pltpu.VMEM(wide, BF16),
            pltpu.VMEM(tall, F32),
            pltpu.VMEM(tall, F32),
            pltpu.VMEM((2, 15, slab, order), F32),
            dma((4,)),
            dma((2, CUTS, 2)),
            dma((3,)),
            dma((3,)),
            dma((2, 15, CUTS)),
            dma((2, 16, CUTS)),
            dma((2, 16)),
            dma((2, 16)),
            dma((2, 15, CUTS)),
            dma((2, 15, CUTS)),
        ],
        compiler_params=pltpu.CompilerParams(
            collective_id=0, has_side_effects=True, vmem_limit_bytes=60 * 1024 * 1024
        ),
        cost_estimate=pl.CostEstimate(flops=19 * 10**9, bytes_accessed=16 * 10**6, transcendentals=10**6),
    )(inputs, first_factor, second_factor, cotangent)
    return pl.pallas_call(
        deliver,
        out_shape=tuple(jax.ShapeDtypeStruct(a.shape, F32) for a in found),
        in_specs=[pl.BlockSpec(memory_space=pl.ANY)] * 3,
        out_specs=[pl.BlockSpec(memory_space=pl.ANY)] * 3,
        scratch_shapes=[pltpu.VMEM(a.shape, F32) for a in found] + [dma((8,)), dma((8,))],
        cost_estimate=pl.CostEstimate(flops=0, bytes_accessed=6 * 10**6, transcendentals=0),
    )(*found)


def solution(mesh):
    placed = (P("tok", "blk"), P("blk", "tok", None), P("blk", "tok", None), P("tok", "blk"))
    return jax.shard_map(
        body,
        mesh=mesh,
        in_specs=placed,
        out_specs=(P("tok", "blk"), P("blk", "tok", None), P("blk", "tok", None)),
        check_vma=False,
    )
```
